32 devices in a mesh: parts: 2 (over x), wide: 16 (over z, y, core).
Axes of the slice: x: 2, y: 2, z: 4, core: 2. Of those that a mesh axis runs over, the one named last changes fastest.
Arguments:
- tokens: bfloat16 [1024, 8192], P('parts', 'wide'), parts along dimension 0, may hold values from -1100 to 1100
- norm_gain: float32 [8192], replicated, may hold values from 0.25 to 1.75
- gate_weight: bfloat16 [16, 2048, 8192], P('wide'), may hold values from -0.0625 to 0.0625
- up_weight: bfloat16 [16, 2048, 8192], P('wide'), may hold values from -0.0625 to 0.0625
- down_weight: bfloat16 [16, 8192, 2048], P('wide'), may hold values from -0.03125 to 0.03125
Outputs:
- layer_output: bfloat16 [1024, 8192], P('parts', 'wide'), parts along dimension 0
The draws below stay inside these ranges and needn't reach their ends.
There are 2 independent parts, one for each index of `parts`. The reference program is written for one: setup_inputs(seed, part) draws one part's arguments, and reference() takes and returns one part's arrays. A program takes and returns all parts, laid end to end along the dimension named above; an argument that names none is the same for every part. Nothing has to cross between parts.
All inputs are finite; a program needn't handle non-finite values.
Results may differ from the reference program's by a relative error of at most 0.0065.
Values may be sent and summed in bfloat16 or wider, within the bound.
A program may use at most 256 MiB of HBM per device.

```python
import math
import jax
import jax.numpy as jnp
from jax import lax

D = 8192
FF = 32768
WSPLIT = 4
ROWS = 512
N_WIDE = 16


def draw_tokens(key, part):
    key_base = jax.random.fold_in(key, 11)
    key_rows = jax.random.fold_in(key, 12)
    key_cols = jax.random.fold_in(key, 13)
    base = jax.random.truncated_normal(key_base, -6.0, 6.0, (ROWS, D), jnp.float32)
    row_scale = jnp.exp(jax.random.uniform(key_rows, (ROWS, 1), jnp.float32, 0.0, math.log(10.0)))
    ramp = jnp.arange(D, dtype=jnp.float32)[None, :] / D
    col_scale = jnp.exp(jax.random.uniform(key_cols, (1, D), jnp.float32, 0.0, math.log(10.0)) + 0.5 * math.log(3.0) * ramp)
    return (base * row_scale * col_scale).astype(jnp.bfloat16)


def shard_levels(stream_key, shape, split, least, high):
    loudness, own = 1.0, jax.random.fold_in(stream_key, 6)
    for position, shards_of in split:
        heights = jnp.exp(jax.random.uniform(jax.random.fold_in(own, position), (shards_of,), jnp.float32, least / len(split), high / len(split)))
        loudness = loudness * jnp.repeat(heights, shape[position] // shards_of).reshape([-1 if axis == position else 1 for axis in range(len(shape))])
    return loudness


def normal_values(own_key, dims, scale, most, shards=(), kind=jnp.bfloat16):
    array = scale * jax.random.normal(own_key, dims, jnp.float32)
    if shards:
        array = array * shard_levels(own_key, dims, shards, -0.22, 0.18)
    return jnp.clip(array, -most, most).astype(kind)


def setup_inputs(seed: int = 0, part: int = 0) -> dict:
    splits = jax.random.split(jax.random.key(seed), 6)
    part_keys = jax.random.split(jax.random.fold_in(splits[5], part), 6)
    tokens = draw_tokens(jax.random.fold_in(jax.random.fold_in(splits[5], part), 71), part)
    norm_gain = jnp.clip(1.0 + 0.15 * jax.random.normal(splits[1], (D,), jnp.float32), 0.25, 1.75)
    gate_weight = normal_values(splits[2], (N_WIDE, D // WSPLIT, FF * WSPLIT // N_WIDE), D ** -0.5, 0.0625, ((0, 16),))
    up_weight = normal_values(splits[3], (N_WIDE, D // WSPLIT, FF * WSPLIT // N_WIDE), D ** -0.5, 0.0625, ((0, 16),))
    down_weight = normal_values(splits[4], (N_WIDE, FF * WSPLIT // N_WIDE, D // WSPLIT), FF ** -0.5, 0.03125, ((0, 16),))
    return dict(tokens=tokens, norm_gain=norm_gain, gate_weight=gate_weight, up_weight=up_weight, down_weight=down_weight)


epsilon = 1e-05

def assemble_in(blocks):
    groups = N_WIDE // WSPLIT
    parted = blocks.reshape(groups, WSPLIT, groups, D // N_WIDE, FF // groups)
    return jnp.transpose(parted, (2, 1, 3, 0, 4)).reshape(D, FF)

def assemble_out(blocks):
    groups = N_WIDE // WSPLIT
    parted = blocks.reshape(groups, WSPLIT, FF // groups, groups, D // N_WIDE)
    return jnp.transpose(parted, (0, 2, 3, 1, 4)).reshape(FF, D)

def reference(tokens, norm_gain, gate_weight, up_weight, down_weight):
    values = tokens.astype(jnp.float32)
    inverse = lax.rsqrt(lax.optimization_barrier(jnp.mean(values * values, axis=1, keepdims=True)) + epsilon)
    normed = (values * inverse * norm_gain).astype(jnp.bfloat16)
    gate_proj = jnp.dot(normed, assemble_in(gate_weight), preferred_element_type=jnp.float32)
    up_proj = jnp.dot(normed, assemble_in(up_weight), preferred_element_type=jnp.float32)
    hidden = (jax.nn.silu(gate_proj) * up_proj).astype(jnp.bfloat16)
    return jnp.dot(hidden, assemble_out(down_weight), preferred_element_type=jnp.float32).astype(jnp.bfloat16)
```

```python
import jax
import jax.numpy as jnp
from jax import lax
from jax.sharding import PartitionSpec as P

WSPLIT = 4
ROW_CHUNKS = 2
UNIT_CHUNKS = 4

epsilon = 1e-05


def partner(block, bit):
    count = lax.axis_size("wide")
    return lax.ppermute(block, "wide", [(i, i ^ (1 << bit)) for i in range(count)])


def shift(block, groups, step, valid):
    route = []
    for h in valid:
        if 0 <= h < groups and 0 <= h + step < groups:
            route += [
                (h * WSPLIT + lane, (h + step) * WSPLIT + lane) for lane in range(WSPLIT)
            ]
    return lax.ppermute(block, "wide", route)


def gather_groups(block, group, groups):
    rows, piece = block.shape
    pieces = jnp.zeros((groups, rows, piece), block.dtype)
    pieces = lax.dynamic_update_index_in_dim(pieces, block, group, 0)
    right = left = block
    for step in range(1, groups):
        right = shift(right, groups, 1, range(groups - 1))
        left = shift(left, groups, -1, range(1, groups))
        low, high = group - step, group + step
        index = lax.broadcasted_iota(jnp.int32, (groups, 1, 1), 0)
        pieces = jnp.where(index == low, right[None], pieces)
        pieces = jnp.where(index == high, left[None], pieces)
    return jnp.concatenate([pieces[h] for h in range(groups)], axis=1)


def scatter_groups(result, group, groups):
    rows, width = result.shape
    piece = width // groups

    def block(index):
        index = jnp.clip(index, 0, groups - 1)
        return lax.dynamic_slice(result, (0, index * piece), (rows, piece))

    last = groups - 1
    right = left = None
    for step in range(last):
        out_right = block(group + last - step)
        out_left = block(group - last + step)
        if right is not None:
            out_right = out_right + right.astype(jnp.float32)
            out_left = out_left + left.astype(jnp.float32)
        right = shift(out_right.astype(jnp.bfloat16), groups, 1, range(step + 1))
        left = shift(out_left.astype(jnp.bfloat16), groups, -1, range(last - step, groups))
    mine = block(group)
    if right is not None:
        mine = mine + right.astype(jnp.float32) + left.astype(jnp.float32)
    return mine.astype(jnp.bfloat16)


def shards(tokens, norm_gain, gate_weight, up_weight, down_weight):
    total = lax.axis_size("wide")
    position = lax.axis_index("wide")
    groups = total // WSPLIT
    rows, piece = tokens.shape
    width = norm_gain.shape[0]
    units = gate_weight.shape[2]
    lane, group = position % WSPLIT, position // WSPLIT
    core, side = position & 1, position >> 1 & 1
    gains = lax.dynamic_index_in_dim(
        norm_gain.reshape(groups, WSPLIT, piece), lane, 1, keepdims=False
    ).reshape(groups * piece)
    values = tokens.astype(jnp.float32)
    squares = jnp.sum(values * values, axis=1)
    for bit in range(total.bit_length() - 1):
        squares = squares + partner(squares, bit)
    inverse = lax.rsqrt(squares[:, None] / width + epsilon)

    chunk_rows = rows // ROW_CHUNKS
    chunk = units // UNIT_CHUNKS
    half, quarter = chunk // 2, chunk // 4
    gate, up, down = gate_weight[0], up_weight[0], down_weight[0]

    def dot(a, weight, start, size):
        return jnp.dot(
            a,
            lax.dynamic_slice(weight, (0, start), (weight.shape[0], size)),
            preferred_element_type=jnp.float32,
        )

    outputs = []
    for r in range(ROW_CHUNKS):
        span = slice(r * chunk_rows, (r + 1) * chunk_rows)
        mine = gather_groups(tokens[span], group, groups)
        normed = (mine.astype(jnp.float32) * inverse[span] * gains).astype(jnp.bfloat16)
        result = None
        for c in range(UNIT_CHUNKS):
            base = c * chunk
            away = base + (1 - core) * half
            near = base + core * half
            sent = near + (1 - side) * quarter
            kept = near + side * quarter
            sums = []
            for weight in (gate, up):
                got = partner(dot(normed, weight, away, half).astype(jnp.bfloat16), 0)
                got = got.astype(jnp.float32)
                got_sent = lax.dynamic_slice(
                    got, (0, (1 - side) * quarter), (chunk_rows, quarter)
                )
                got_kept = lax.dynamic_slice(got, (0, side * quarter), (chunk_rows, quarter))
                out = (dot(normed, weight, sent, quarter) + got_sent).astype(jnp.bfloat16)
                back = partner(out, 1)
                sums.append(
                    dot(normed, weight, kept, quarter) + got_kept + back.astype(jnp.float32)
                )
            hidden = (jax.nn.silu(sums[0]) * sums[1]).astype(jnp.bfloat16)
            for bit in (1, 0):
                received = partner(hidden, bit)
                upper = position >> bit & 1 == 1
                hidden = jnp.concatenate(
                    [jnp.where(upper, received, hidden), jnp.where(upper, hidden, received)],
                    axis=1,
                )
            term = jnp.dot(
                hidden, down[base : base + chunk], preferred_element_type=jnp.float32
            )
            result = term if result is None else result + term
        outputs.append(scatter_groups(result, group, groups))
    return jnp.concatenate(outputs, axis=0)


def solution(mesh):
    placed = (
        P("parts", "wide"),
        P(),
        P("wide", None, None),
        P("wide", None, None),
        P("wide", None, None),
    )
    return jax.shard_map(
        shards, mesh=mesh, in_specs=placed, out_specs=P("parts", "wide"), check_vma=False
    )
```

```python
import jax
import jax.numpy as jnp
from jax import lax
from jax.sharding import PartitionSpec as P

WSPLIT = 4
ROW_CHUNKS = 2
UNIT_CHUNKS = 4

epsilon = 1e-05


def partner(block, bit):
    count = lax.axis_size("wide")
    return lax.ppermute(block, "wide", [(i, i ^ (1 << bit)) for i in range(count)])


def shift(block, groups, step, valid):
    route = []
    for h in valid:
        if 0 <= h < groups and 0 <= h + step < groups:
            route += [
                (h * WSPLIT + lane, (h + step) * WSPLIT + lane) for lane in range(WSPLIT)
            ]
    return lax.ppermute(block, "wide", route)


def gather_groups(block, group, groups):
    rows, piece = block.shape
    pieces = jnp.zeros((groups, rows, piece), block.dtype)
    pieces = lax.dynamic_update_index_in_dim(pieces, block, group, 0)
    right = left = block
    for step in range(1, groups):
        right = shift(right, groups, 1, range(groups - 1))
        left = shift(left, groups, -1, range(1, groups))
        low, high = group - step, group + step
        index = lax.broadcasted_iota(jnp.int32, (groups, 1, 1), 0)
        pieces = jnp.where(index == low, right[None], pieces)
        pieces = jnp.where(index == high, left[None], pieces)
    return jnp.concatenate([pieces[h] for h in range(groups)], axis=1)


def scatter_groups(result, group, groups):
    rows, width = result.shape
    piece = width // groups

    def block(index):
        index = jnp.clip(index, 0, groups - 1)
        return lax.dynamic_slice(result, (0, index * piece), (rows, piece))

    last = groups - 1
    right = left = None
    for step in range(last):
        out_right = block(group + last - step)
        out_left = block(group - last + step)
        if right is not None:
            out_right = out_right + right.astype(jnp.float32)
            out_left = out_left + left.astype(jnp.float32)
        right = shift(out_right.astype(jnp.bfloat16), groups, 1, range(step + 1))
        left = shift(out_left.astype(jnp.bfloat16), groups, -1, range(last - step, groups))
    mine = block(group)
    if right is not None:
        mine = mine + right.astype(jnp.float32) + left.astype(jnp.float32)
    return mine.astype(jnp.bfloat16)


def shards(tokens, norm_gain, gate_weight, up_weight, down_weight):
    total = lax.axis_size("wide")
    position = lax.axis_index("wide")
    groups = total // WSPLIT
    rows, piece = tokens.shape
    width = norm_gain.shape[0]
    units = gate_weight.shape[2]
    lane, group = position % WSPLIT, position // WSPLIT
    core, side = position & 1, position >> 1 & 1
    gains = lax.dynamic_index_in_dim(
        norm_gain.reshape(groups, WSPLIT, piece), lane, 1, keepdims=False
    ).reshape(groups * piece)
    values = tokens.astype(jnp.float32)
    squares = jnp.sum(values * values, axis=1)
    for bit in range(total.bit_length() - 1):
        squares = squares + partner(squares, bit)
    inverse = lax.rsqrt(squares[:, None] / width + epsilon)

    chunk_rows = rows // ROW_CHUNKS
    chunk = units // UNIT_CHUNKS
    half, quarter = chunk // 2, chunk // 4
    gate, up, down = gate_weight[0], up_weight[0], down_weight[0]

    def dot(a, weight, start, size):
        return jnp.dot(
            a,
            lax.dynamic_slice(weight, (0, start), (weight.shape[0], size)),
            preferred_element_type=jnp.float32,
        )

    stages = [(r, c) for r in range(ROW_CHUNKS) for c in range(UNIT_CHUNKS)]
    count = len(stages)
    previous = [tokens]
    normed, state, hiddens = {}, {}, {}
    results = [None] * ROW_CHUNKS
    outputs = [None] * ROW_CHUNKS

    def ordered(*values):
        tied, _ = lax.optimization_barrier((values, tuple(previous)))
        return tied

    def gather(r):
        (block,) = ordered(tokens[r * chunk_rows : (r + 1) * chunk_rows])
        mine = gather_groups(block, group, groups)
        scale = inverse[r * chunk_rows : (r + 1) * chunk_rows]
        normed[r] = (mine.astype(jnp.float32) * scale * gains).astype(jnp.bfloat16)

    def project(k):
        r, c = stages[k]
        (a,) = ordered(normed[r])
        base = c * chunk
        away = base + (1 - core) * half
        near = base + core * half
        sent = near + (1 - side) * quarter
        kept = near + side * quarter
        both = (gate, up)
        gone = [dot(a, w, away, half).astype(jnp.bfloat16) for w in both]
        got = [partner(g, 0) for g in gone]
        a, _ = lax.optimization_barrier((a, tuple(gone)))
        keep = [dot(a, w, kept, quarter) for w in both]
        a, _ = lax.optimization_barrier((a, tuple(keep)))
        out = []
        for w, g in zip(both, got):
            part = lax.dynamic_slice(g, (0, (1 - side) * quarter), (chunk_rows, quarter))
            out.append((dot(a, w, sent, quarter) + part.astype(jnp.float32)).astype(jnp.bfloat16))
        back = [partner(o, 1) for o in out]
        mine = [
            lax.dynamic_slice(g, (0, side * quarter), (chunk_rows, quarter)) for g in got
        ]
        state[k] = keep, mine, back
        previous[:] = out

    def activate(k):
        keep, mine, back = state.pop(k)
        keep = ordered(*keep)
        sums = [
            x + y.astype(jnp.float32) + z.astype(jnp.float32)
            for x, y, z in zip(keep, mine, back)
        ]
        hidden = (jax.nn.silu(sums[0]) * sums[1]).astype(jnp.bfloat16)
        previous[:] = [hidden]
        for bit in (1, 0):
            received = partner(hidden, bit)
            upper = position >> bit & 1 == 1
            hidden = jnp.concatenate(
                [jnp.where(upper, received, hidden), jnp.where(upper, hidden, received)],
                axis=1,
            )
        hiddens[k] = hidden

    def contract(k):
        r, c = stages[k]
        (hidden,) = ordered(hiddens.pop(k))
        term = jnp.dot(
            hidden, down[c * chunk : (c + 1) * chunk], preferred_element_type=jnp.float32
        )
        results[r] = term if results[r] is None else results[r] + term
        previous[:] = [results[r]]
        if c == UNIT_CHUNKS - 1:
            outputs[r] = scatter_groups(results[r], group, groups)

    gather(0)
    for k in range(count + 2):
        if k < count:
            project(k)
            r, c = stages[k]
            if c == 0 and r + 1 < ROW_CHUNKS:
                gather(r + 1)
        if 1 <= k <= count:
            activate(k - 1)
        if k >= 2:
            contract(k - 2)
    return jnp.concatenate(outputs, axis=0)


def solution(mesh):
    placed = (
        P("parts", "wide"),
        P(),
        P("wide", None, None),
        P("wide", None, None),
        P("wide", None, None),
    )
    return jax.shard_map(
        shards, mesh=mesh, in_specs=placed, out_specs=P("parts", "wide"), check_vma=False
    )
```

```python
import jax
import jax.numpy as jnp
from jax import lax
from jax.experimental import pallas as pl
from jax.experimental.pallas import tpu as pltpu
from jax.sharding import PartitionSpec as P

WSPLIT = 4
ROW_CHUNKS = 2
UNIT_CHUNKS = 4

epsilon = 1e-05


def partner(block, bit):
    count = lax.axis_size("wide")
    return lax.ppermute(block, "wide", [(i, i ^ (1 << bit)) for i in range(count)])


def shift(block, groups, step, valid):
    route = []
    for h in valid:
        if 0 <= h < groups and 0 <= h + step < groups:
            route += [
                (h * WSPLIT + lane, (h + step) * WSPLIT + lane) for lane in range(WSPLIT)
            ]
    return lax.ppermute(block, "wide", route)


def gather_groups(block, group, groups):
    rows, piece = block.shape
    pieces = jnp.zeros((groups, rows, piece), block.dtype)
    pieces = lax.dynamic_update_index_in_dim(pieces, block, group, 0)
    right = left = block
    for step in range(1, groups):
        right = shift(right, groups, 1, range(groups - 1))
        left = shift(left, groups, -1, range(1, groups))
        low, high = group - step, group + step
        index = lax.broadcasted_iota(jnp.int32, (groups, 1, 1), 0)
        pieces = jnp.where(index == low, right[None], pieces)
        pieces = jnp.where(index == high, left[None], pieces)
    return jnp.concatenate([pieces[h] for h in range(groups)], axis=1)


def scatter_groups(result, group, groups):
    rows, width = result.shape
    piece = width // groups

    def block(index):
        index = jnp.clip(index, 0, groups - 1)
        return lax.dynamic_slice(result, (0, index * piece), (rows, piece))

    last = groups - 1
    right = left = None
    for step in range(last):
        out_right = block(group + last - step)
        out_left = block(group - last + step)
        if right is not None:
            out_right = out_right + right.astype(jnp.float32)
            out_left = out_left + left.astype(jnp.float32)
        right = shift(out_right.astype(jnp.bfloat16), groups, 1, range(step + 1))
        left = shift(out_left.astype(jnp.bfloat16), groups, -1, range(last - step, groups))
    mine = block(group)
    if right is not None:
        mine = mine + right.astype(jnp.float32) + left.astype(jnp.float32)
    return mine.astype(jnp.bfloat16)


def product(a, weight):
    return jnp.dot(a, weight, preferred_element_type=jnp.float32)


def params(flops, bytes_accessed):
    return dict(
        compiler_params=pltpu.CompilerParams(vmem_limit_bytes=40 * 2**20),
        cost_estimate=pl.CostEstimate(
            flops=flops, bytes_accessed=bytes_accessed, transcendentals=0
        ),
    )


def away_kernel(order, a, gate, up, gate_out, up_out):
    gate_out[...] = product(a[...], gate[0]).astype(jnp.bfloat16)
    up_out[...] = product(a[...], up[0]).astype(jnp.bfloat16)


def project_away(a, gate, up, order, tile):
    m, k = a.shape
    n = order.shape[0]
    weight = pl.BlockSpec((1, k, tile), lambda j, order: (0, 0, order[j]))
    out = pl.BlockSpec((m, tile), lambda j, order: (0, j))
    return pl.pallas_call(
        away_kernel,
        grid_spec=pltpu.PrefetchScalarGridSpec(
            num_scalar_prefetch=1,
            grid=(n,),
            in_specs=[pl.BlockSpec((m, k), lambda j, order: (0, 0)), weight, weight],
            out_specs=[out, out],
        ),
        out_shape=[jax.ShapeDtypeStruct((m, n * tile), jnp.bfloat16)] * 2,
        **params(4 * m * k * n * tile, 4 * k * n * tile),
    )(order, a, gate, up)


def near_kernel(n, order, place, a, gate, up, gate_got, up_got, *outs):
    j = pl.program_id(0)
    gate_sum = product(a[...], gate[0]) + gate_got[...].astype(jnp.float32)
    up_sum = product(a[...], up[0]) + up_got[...].astype(jnp.float32)

    @pl.when(j < n)
    def _():
        outs[0][...] = gate_sum.astype(jnp.bfloat16)
        outs[1][...] = up_sum.astype(jnp.bfloat16)

    @pl.when(j >= n)
    def _():
        outs[2][...] = gate_sum
        outs[3][...] = up_sum


def project_near(a, gate, up, gate_got, up_got, order, place, tile):
    m, k = a.shape
    n = order.shape[0] // 2
    weight = pl.BlockSpec((1, k, tile), lambda j, order, place: (0, 0, order[j]))
    got = pl.BlockSpec((m, tile), lambda j, order, place: (0, place[j]))
    sent = pl.BlockSpec((m, tile), lambda j, order, place: (0, jnp.minimum(j, n - 1)))
    kept = pl.BlockSpec((m, tile), lambda j, order, place: (0, jnp.maximum(j - n, 0)))
    return pl.pallas_call(
        lambda *refs: near_kernel(n, *refs),
        grid_spec=pltpu.PrefetchScalarGridSpec(
            num_scalar_prefetch=2,
            grid=(2 * n,),
            in_specs=[
                pl.BlockSpec((m, k), lambda j, order, place: (0, 0)), weight, weight, got, got,
            ],
            out_specs=[sent, sent, kept, kept],
        ),
        out_shape=[jax.ShapeDtypeStruct((m, n * tile), jnp.bfloat16)] * 2
        + [jax.ShapeDtypeStruct((m, n * tile), jnp.float32)] * 2,
        **params(8 * m * k * n * tile, 8 * k * n * tile),
    )(order, place, a, gate, up, gate_got, up_got)


def down_kernel(a, weight, *refs):
    term = product(a[...], weight[0])
    if len(refs) == 2:
        term = term + refs[0][...]
    refs[-1][...] = term


def project_down(a, weight, chunk_index, total):
    m, k = a.shape
    width = weight.shape[2]
    tile = min(512, width)
    out = pl.BlockSpec((m, tile), lambda j: (0, j))
    adds = [] if total is None else [total]
    return pl.pallas_call(
        down_kernel,
        grid=(width // tile,),
        in_specs=[
            pl.BlockSpec((m, k), lambda j: (0, 0)),
            pl.BlockSpec((1, k, tile), lambda j: (0, chunk_index, j)),
        ]
        + [out] * len(adds),
        out_specs=out,
        out_shape=jax.ShapeDtypeStruct((m, width), jnp.float32),
        **params(2 * m * k * width, 2 * k * width),
    )(a, weight, *adds)


def shards(tokens, norm_gain, gate_weight, up_weight, down_weight):
    total = lax.axis_size("wide")
    position = lax.axis_index("wide")
    groups = total // WSPLIT
    rows, piece = tokens.shape
    width = norm_gain.shape[0]
    units = gate_weight.shape[2]
    lane, group = position % WSPLIT, position // WSPLIT
    core, side = position & 1, position >> 1 & 1
    gains = lax.dynamic_index_in_dim(
        norm_gain.reshape(groups, WSPLIT, piece), lane, 1, keepdims=False
    ).reshape(groups * piece)
    values = tokens.astype(jnp.float32)
    squares = jnp.sum(values * values, axis=1)
    for bit in range(total.bit_length() - 1):
        squares = squares + partner(squares, bit)
    inverse = lax.rsqrt(squares[:, None] / width + epsilon)

    chunk_rows = rows // ROW_CHUNKS
    unit_chunks = max(1, min(UNIT_CHUNKS, units // 512))
    chunk = units // unit_chunks
    half, quarter = chunk // 2, chunk // 4
    tile = min(256, quarter)
    per_half, per_quarter = half // tile, quarter // tile

    stages = [(r, c) for r in range(ROW_CHUNKS) for c in range(unit_chunks)]
    count = len(stages)
    previous = [tokens]
    normed, gots, state, hiddens = {}, {}, {}, {}
    results = [None] * ROW_CHUNKS
    outputs = [None] * ROW_CHUNKS

    def ordered(*values):
        tied, _ = lax.optimization_barrier((values, tuple(previous)))
        return tied

    def gather(r):
        (block,) = ordered(tokens[r * chunk_rows : (r + 1) * chunk_rows])
        mine = gather_groups(block, group, groups)
        scale = inverse[r * chunk_rows : (r + 1) * chunk_rows]
        normed[r] = (mine.astype(jnp.float32) * scale * gains).astype(jnp.bfloat16)

    def away(k):
        r, c = stages[k]
        (a,) = ordered(normed[r])
        first = (c * chunk + (1 - core) * half) // tile
        order = (first + jnp.arange(per_half)).astype(jnp.int32)
        gone = project_away(a, gate_weight, up_weight, order, tile)
        previous[:] = gone
        gots[k] = [partner(g, 0) for g in gone]

    def near(k):
        r, c = stages[k]
        (a,) = ordered(normed[r])
        steps = jnp.arange(per_quarter)
        place = jnp.concatenate(
            [(1 - side) * per_quarter + steps, side * per_quarter + steps]
        ).astype(jnp.int32)
        order = place + ((c * chunk + core * half) // tile).astype(jnp.int32)
        outs = project_near(a, gate_weight, up_weight, *gots.pop(k), order, place, tile)
        previous[:] = outs
        state[k] = outs[2:], [partner(o, 1) for o in outs[:2]]

    def activate(k):
        keep, back = state.pop(k)
        keep = ordered(*keep)
        sums = [x + y.astype(jnp.float32) for x, y in zip(keep, back)]
        hidden = (jax.nn.silu(sums[0]) * sums[1]).astype(jnp.bfloat16)
        previous[:] = [hidden]
        for bit in (1, 0):
            received = partner(hidden, bit)
            upper = position >> bit & 1 == 1
            hidden = jnp.concatenate(
                [jnp.where(upper, received, hidden), jnp.where(upper, hidden, received)],
                axis=1,
            )
        hiddens[k] = hidden

    def contract(k):
        r, c = stages[k]
        (hidden,) = ordered(hiddens.pop(k))
        results[r] = project_down(hidden, down_weight, c, results[r])
        previous[:] = [results[r]]
        if c == unit_chunks - 1:
            outputs[r] = scatter_groups(results[r], group, groups)

    gather(0)
    away(0)
    for k in range(count + 2):
        if k + 1 < count:
            away(k + 1)
        if k < count:
            near(k)
            r, c = stages[k]
            if c == 0 and r + 1 < ROW_CHUNKS:
                gather(r + 1)
        if 1 <= k <= count:
            activate(k - 1)
        if k >= 2:
            contract(k - 2)
    return jnp.concatenate(outputs, axis=0)


def solution(mesh):
    placed = (
        P("parts", "wide"),
        P(),
        P("wide", None, None),
        P("wide", None, None),
        P("wide", None, None),
    )
    return jax.shard_map(
        shards, mesh=mesh, in_specs=placed, out_specs=P("parts", "wide"), check_vma=False
    )
```

```python
import jax
import jax.numpy as jnp
from jax import lax
from jax.experimental import pallas as pl
from jax.experimental.pallas import tpu as pltpu
from jax.sharding import PartitionSpec as P

WSPLIT = 4
ROW_CHUNKS = 1
UNIT_CHUNKS = 8

epsilon = 1e-05


def partner(block, bit):
    count = lax.axis_size("wide")
    return lax.ppermute(block, "wide", [(i, i ^ (1 << bit)) for i in range(count)])


def shift(block, groups, step, valid):
    route = []
    for h in valid:
        if 0 <= h < groups and 0 <= h + step < groups:
            route += [
                (h * WSPLIT + lane, (h + step) * WSPLIT + lane) for lane in range(WSPLIT)
            ]
    return lax.ppermute(block, "wide", route)


def gather_groups(block, group, groups):
    rows, piece = block.shape
    pieces = jnp.zeros((groups, rows, piece), block.dtype)
    pieces = lax.dynamic_update_index_in_dim(pieces, block, group, 0)
    right = left = block
    for step in range(1, groups):
        right = shift(right, groups, 1, range(groups - 1))
        left = shift(left, groups, -1, range(1, groups))
        low, high = group - step, group + step
        index = lax.broadcasted_iota(jnp.int32, (groups, 1, 1), 0)
        pieces = jnp.where(index == low, right[None], pieces)
        pieces = jnp.where(index == high, left[None], pieces)
    return jnp.concatenate([pieces[h] for h in range(groups)], axis=1)


def scatter_groups(result, group, groups):
    rows, width = result.shape
    piece = width // groups

    def block(index):
        index = jnp.clip(index, 0, groups - 1)
        return lax.dynamic_slice(result, (0, index * piece), (rows, piece))

    last = groups - 1
    right = left = None
    for step in range(last):
        out_right = block(group + last - step)
        out_left = block(group - last + step)
        if right is not None:
            out_right = out_right + right.astype(jnp.float32)
            out_left = out_left + left.astype(jnp.float32)
        right = shift(out_right.astype(jnp.bfloat16), groups, 1, range(step + 1))
        left = shift(out_left.astype(jnp.bfloat16), groups, -1, range(last - step, groups))
    mine = block(group)
    if right is not None:
        mine = mine + right.astype(jnp.float32) + left.astype(jnp.float32)
    return mine.astype(jnp.bfloat16)


def product(a, weight):
    return jnp.dot(a, weight, preferred_element_type=jnp.float32)


def params(flops, bytes_accessed):
    return dict(
        compiler_params=pltpu.CompilerParams(vmem_limit_bytes=40 * 2**20),
        cost_estimate=pl.CostEstimate(
            flops=flops, bytes_accessed=bytes_accessed, transcendentals=0
        ),
    )


def away_kernel(order, a, gate, up, gate_out, up_out):
    gate_out[...] = product(a[...], gate[0]).astype(jnp.bfloat16)
    up_out[...] = product(a[...], up[0]).astype(jnp.bfloat16)


def project_away(a, gate, up, order, tile):
    m, k = a.shape
    n = order.shape[0]
    weight = pl.BlockSpec((1, k, tile), lambda j, order: (0, 0, order[j]))
    out = pl.BlockSpec((m, tile), lambda j, order: (0, j))
    return pl.pallas_call(
        away_kernel,
        grid_spec=pltpu.PrefetchScalarGridSpec(
            num_scalar_prefetch=1,
            grid=(n,),
            in_specs=[pl.BlockSpec((m, k), lambda j, order: (0, 0)), weight, weight],
            out_specs=[out, out],
        ),
        out_shape=[jax.ShapeDtypeStruct((m, n * tile), jnp.bfloat16)] * 2,
        **params(4 * m * k * n * tile, 4 * k * n * tile),
    )(order, a, gate, up)


def near_kernel(n, order, place, a, gate, up, gate_got, up_got, *outs):
    j = pl.program_id(0)
    gate_sum = product(a[...], gate[0]) + gate_got[...].astype(jnp.float32)
    up_sum = product(a[...], up[0]) + up_got[...].astype(jnp.float32)

    @pl.when(j < n)
    def _():
        outs[0][...] = gate_sum.astype(jnp.bfloat16)
        outs[1][...] = up_sum.astype(jnp.bfloat16)

    @pl.when(j >= n)
    def _():
        outs[2][...] = gate_sum
        outs[3][...] = up_sum


def project_near(a, gate, up, gate_got, up_got, order, place, tile):
    m, k = a.shape
    n = order.shape[0] // 2
    weight = pl.BlockSpec((1, k, tile), lambda j, order, place: (0, 0, order[j]))
    got = pl.BlockSpec((m, tile), lambda j, order, place: (0, place[j]))
    sent = pl.BlockSpec((m, tile), lambda j, order, place: (0, jnp.minimum(j, n - 1)))
    kept = pl.BlockSpec((m, tile), lambda j, order, place: (0, jnp.maximum(j - n, 0)))
    return pl.pallas_call(
        lambda *refs: near_kernel(n, *refs),
        grid_spec=pltpu.PrefetchScalarGridSpec(
            num_scalar_prefetch=2,
            grid=(2 * n,),
            in_specs=[
                pl.BlockSpec((m, k), lambda j, order, place: (0, 0)), weight, weight, got, got,
            ],
            out_specs=[sent, sent, kept, kept],
        ),
        out_shape=[jax.ShapeDtypeStruct((m, n * tile), jnp.bfloat16)] * 2
        + [jax.ShapeDtypeStruct((m, n * tile), jnp.float32)] * 2,
        **params(8 * m * k * n * tile, 8 * k * n * tile),
    )(order, place, a, gate, up, gate_got, up_got)


def down_kernel(a, weight, *refs):
    term = product(a[...], weight[0])
    if len(refs) == 2:
        term = term + refs[0][...]
    refs[-1][...] = term


def project_down(a, weight, chunk_index, total):
    m, k = a.shape
    width = weight.shape[2]
    tile = min(512, width)
    out = pl.BlockSpec((m, tile), lambda j: (0, j))
    adds = [] if total is None else [total]
    return pl.pallas_call(
        down_kernel,
        grid=(width // tile,),
        in_specs=[
            pl.BlockSpec((m, k), lambda j: (0, 0)),
            pl.BlockSpec((1, k, tile), lambda j: (0, chunk_index, j)),
        ]
        + [out] * len(adds),
        out_specs=out,
        out_shape=jax.ShapeDtypeStruct((m, width), jnp.float32),
        **params(2 * m * k * width, 2 * k * width),
    )(a, weight, *adds)


def shards(tokens, norm_gain, gate_weight, up_weight, down_weight):
    total = lax.axis_size("wide")
    position = lax.axis_index("wide")
    groups = total // WSPLIT
    rows, piece = tokens.shape
    width = norm_gain.shape[0]
    units = gate_weight.shape[2]
    lane, group = position % WSPLIT, position // WSPLIT
    core, side = position & 1, position >> 1 & 1
    gains = lax.dynamic_index_in_dim(
        norm_gain.reshape(groups, WSPLIT, piece), lane, 1, keepdims=False
    ).reshape(groups * piece)
    values = tokens.astype(jnp.float32)
    squares = jnp.sum(values * values, axis=1)
    for bit in range(total.bit_length() - 1):
        squares = squares + partner(squares, bit)
    inverse = lax.rsqrt(squares[:, None] / width + epsilon)

    chunk_rows = rows // ROW_CHUNKS
    unit_chunks = max(1, min(UNIT_CHUNKS, units // 512))
    chunk = units // unit_chunks
    half, quarter = chunk // 2, chunk // 4
    tile = min(256, quarter)
    per_half, per_quarter = half // tile, quarter // tile

    stages = [(r, c) for r in range(ROW_CHUNKS) for c in range(unit_chunks)]
    count = len(stages)
    previous = [tokens]
    normed, gots, state, hiddens = {}, {}, {}, {}
    results = [None] * ROW_CHUNKS
    outputs = [None] * ROW_CHUNKS

    def ordered(*values):
        tied, _ = lax.optimization_barrier((values, tuple(previous)))
        return tied

    def gather(r):
        (block,) = ordered(tokens[r * chunk_rows : (r + 1) * chunk_rows])
        mine = gather_groups(block, group, groups)
        scale = inverse[r * chunk_rows : (r + 1) * chunk_rows]
        normed[r] = (mine.astype(jnp.float32) * scale * gains).astype(jnp.bfloat16)

    def away(k):
        r, c = stages[k]
        (a,) = ordered(normed[r])
        first = (c * chunk + (1 - core) * half) // tile
        order = (first + jnp.arange(per_half)).astype(jnp.int32)
        gone = project_away(a, gate_weight, up_weight, order, tile)
        previous[:] = gone
        gots[k] = [partner(g, 0) for g in gone]

    def near(k):
        r, c = stages[k]
        (a,) = ordered(normed[r])
        steps = jnp.arange(per_quarter)
        place = jnp.concatenate(
            [(1 - side) * per_quarter + steps, side * per_quarter + steps]
        ).astype(jnp.int32)
        order = place + ((c * chunk + core * half) // tile).astype(jnp.int32)
        outs = project_near(a, gate_weight, up_weight, *gots.pop(k), order, place, tile)
        previous[:] = outs
        state[k] = outs[2:], [partner(o, 1) for o in outs[:2]]

    def activate(k):
        keep, back = state.pop(k)
        keep = ordered(*keep)
        sums = [x + y.astype(jnp.float32) for x, y in zip(keep, back)]
        hidden = (jax.nn.silu(sums[0]) * sums[1]).astype(jnp.bfloat16)
        previous[:] = [hidden]
        for bit in (1, 0):
            received = partner(hidden, bit)
            upper = position >> bit & 1 == 1
            hidden = jnp.concatenate(
                [jnp.where(upper, received, hidden), jnp.where(upper, hidden, received)],
                axis=1,
            )
        hiddens[k] = hidden

    def contract(k):
        r, c = stages[k]
        (hidden,) = ordered(hiddens.pop(k))
        results[r] = project_down(hidden, down_weight, c, results[r])
        previous[:] = [results[r]]
        if c == unit_chunks - 1:
            outputs[r] = scatter_groups(results[r], group, groups)

    gather(0)
    away(0)
    for k in range(count + 2):
        if k + 1 < count:
            away(k + 1)
        if k < count:
            near(k)
            r, c = stages[k]
            if c == 0 and r + 1 < ROW_CHUNKS:
                gather(r + 1)
        if 1 <= k <= count:
            activate(k - 1)
        if k >= 2:
            contract(k - 2)
    return jnp.concatenate(outputs, axis=0)


def solution(mesh):
    placed = (
        P("parts", "wide"),
        P(),
        P("wide", None, None),
        P("wide", None, None),
        P("wide", None, None),
    )
    return jax.shard_map(
        shards, mesh=mesh, in_specs=placed, out_specs=P("parts", "wide"), check_vma=False
    )
```
